256 devices in a mesh: layer: 4 (over y), expert: 32 (over x, z), dp: 2 (over core).
Axes of the slice: x: 4, y: 4, z: 8, core: 2. Of those that a mesh axis runs over, the one named last changes fastest.
Arguments:
- tokens: bfloat16 [16384, 2304], P(('expert', 'dp')), may hold values from -6 to 6
- expert_ids: int32 [16384], P(('expert', 'dp')), may hold values from 0 to 31, as said below
- slot_ids: int32 [16384], P(('expert', 'dp')), may hold values from 0 to 15, as said below
- live_mask: int32 [16384], P(('expert', 'dp')), may hold values from 0 to 1
- w_enc: bfloat16 [32, 2304, 2048], P('expert', None, 'layer'), may hold values from -0.125 to 0.125
- b_enc: float32 [32, 2048], P('expert', 'layer'), may hold values from -3 to 3
- w_dec: bfloat16 [2, 32, 2048, 2304], P(None, 'expert', 'layer'), may hold values from -0.125 to 0.125
- b_dec: float32 [2, 2304], P(None, 'layer'), may hold values from -3 to 3
- targets: bfloat16 [2, 16384, 2304], P(None, ('expert', 'dp'), 'layer'), may hold values from -6 to 6
Outputs:
- recon: bfloat16 [2, 16384, 2304], P(None, ('expert', 'dp'), 'layer')
- grad_w_enc: bfloat16 [32, 2304, 2048], P('expert', 'dp', 'layer')
- grad_b_enc: float32 [32, 2048], P('expert', ('layer', 'dp'))
- grad_w_dec: bfloat16 [2, 32, 2048, 2304], P(None, 'expert', 'layer', 'dp')
- grad_b_dec: float32 [2, 2304], P(None, 'layer')
The draws below stay inside these ranges and needn't reach their ends.
Inputs may be any that keep to these rules, and one draw needn't show every extreme that they name: `expert_ids`: the 256 tokens of one block name any expert at most 16 times; in every draw one expert is named exactly 16 times by every block. `slot_ids`: tokens of one block that name the same expert have distinct slots.
All inputs are finite; a program needn't handle non-finite values.
Results may differ from the reference program's by a relative error of at most 0.01.
Values may be sent and summed in bfloat16 or wider, within the bound.
No kernel may reach another device: no remote copies, remote signals or barrier semaphores. Data moves between devices by JAX's collectives and lax.ppermute only.
A program may use at most 128 MiB of HBM per device.

```python
import math
import jax
import jax.numpy as jnp
from jax import lax

D = 2304
LAT = 2048
TGT = 2
TOK_DEV = 256
EXPERTS = 32
BLOCKS = 64
TOKENS = 16384
CAP = 16
N_LAYER = 4


def route_cells(key):
    base = jax.random.fold_in(key, 7301)
    busiest = jax.random.randint(jax.random.fold_in(base, 1), (), 0, EXPERTS)
    block_keys = jax.random.split(jax.random.fold_in(base, 2), BLOCKS)
    total_cells = EXPERTS * CAP

    def one_block(block_key):
        key_order, key_second, key_tokens = jax.random.split(block_key, 3)
        cell_ids = jnp.arange(total_cells, dtype=jnp.int32)
        owner_id = cell_ids // CAP
        second = jax.random.randint(key_second, (), 0, EXPERTS)
        tier_rank = jnp.where(owner_id == busiest, 0, jnp.where(owner_id == second, 1, 2)).astype(jnp.int32)
        cell_rank = jnp.argsort(jax.random.permutation(key_order, total_cells)).astype(jnp.int32)
        cell_order = jnp.argsort(tier_rank * total_cells + cell_rank).astype(jnp.int32)
        chosen = cell_order[:TOK_DEV]
        shuffled = chosen[jax.random.permutation(key_tokens, TOK_DEV)]
        return (shuffled // CAP, shuffled % CAP)
    experts_all, slots_all = jax.vmap(one_block)(block_keys)
    return (experts_all.reshape(TOKENS).astype(jnp.int32), slots_all.reshape(TOKENS).astype(jnp.int32))


def draw_expert_ids(key, part):
    return route_cells(key)[0]


def draw_slot_ids(key, part):
    return route_cells(key)[1]


def draw_live_mask(key, part):
    lengths = jax.random.randint(jax.random.fold_in(key, 9157), (BLOCKS,), TOK_DEV // 4, TOK_DEV + 1)
    positions = jnp.arange(TOK_DEV, dtype=jnp.int32)
    return (positions[None, :] < lengths[:, None]).astype(jnp.int32).reshape(TOKENS)


def level_of(rng, dims, cuts, low, high):
    factor_of = 1.0
    for position, parts in cuts:
        heights = jax.random.uniform(jax.random.fold_in(jax.random.fold_in(rng, 6), position), (parts,), jnp.float32, low / len(cuts), high / len(cuts))
        factor_of = factor_of * jnp.repeat(jnp.exp(heights), dims[position] // parts).reshape((-1,) + (1,) * (len(dims) - 1 - position))
    return factor_of


def centred(rng, extent, width, limit, cuts=(), kind=jnp.bfloat16):
    array = width * jax.random.normal(rng, extent, jnp.float32)
    if cuts:
        array = array * level_of(rng, extent, cuts, -0.22, 0.18)
    return jnp.clip(array, -limit, limit).astype(kind)


def setup_inputs(seed: int = 0) -> dict:
    key_list = jax.random.split(jax.random.key(seed), 10)
    tokens = centred(key_list[0], (TOKENS, D), 1.0, 6.0, ((0, 64),))
    expert_ids = draw_expert_ids(jax.random.fold_in(key_list[9], 71), 0)
    slot_ids = draw_slot_ids(jax.random.fold_in(key_list[9], 71), 0)
    live_mask = draw_live_mask(jax.random.fold_in(key_list[9], 71), 0)
    w_enc = centred(key_list[4], (EXPERTS, D, LAT), D ** -0.5, 0.125, ((0, 32), (2, 4)))
    b_enc = centred(key_list[5], (EXPERTS, LAT), 0.5, 3.0, ((0, 32), (1, 4)), jnp.float32)
    w_dec = centred(key_list[6], (TGT, EXPERTS, LAT, D), LAT ** -0.5, 0.125, ((1, 32), (2, 4)))
    b_dec = centred(key_list[7], (TGT, D), 0.5, 3.0, ((1, 4),), jnp.float32)
    targets = centred(key_list[8], (TGT, TOKENS, D), 1.0, 6.0, ((1, 64), (2, 4)))
    return dict(tokens=tokens, expert_ids=expert_ids, slot_ids=slot_ids, live_mask=live_mask, w_enc=w_enc, b_enc=b_enc, w_dec=w_dec, b_dec=b_dec, targets=targets)


def reference(tokens, expert_ids, slot_ids, live_mask, w_enc, b_enc, w_dec, b_dec, targets):
    coef = 2.0 / math.sqrt(TOK_DEV)
    rows_expert = BLOCKS * CAP
    quarter = LAT // N_LAYER
    token_ids = jnp.arange(TOKENS, dtype=jnp.int32)
    row_ids = (token_ids // TOK_DEV * CAP + slot_ids).astype(jnp.int32)
    row_table = jnp.full((EXPERTS, rows_expert), TOKENS, jnp.int32).at[expert_ids, row_ids].set(token_ids)
    tokens_pad = jnp.concatenate([tokens, jnp.zeros((1, D), tokens.dtype)], axis=0)
    targets_pad = jnp.concatenate([targets, jnp.zeros((TGT, 1, D), targets.dtype)], axis=1)
    live_pad = jnp.concatenate([live_mask, jnp.zeros((1,), jnp.int32)]).astype(jnp.float32)

    def one_expert(carry_state, expert):
        recon_out, bias_total = carry_state
        expert_rows = row_table[expert]
        inputs = tokens_pad[expert_rows]
        pre_act = jnp.dot(inputs, w_enc[expert], preferred_element_type=jnp.float32) + b_enc[expert][None, :]
        active = jnp.maximum(pre_act, 0.0)
        latents = (active * active).astype(jnp.bfloat16)
        rebuilt = []
        for target in range(TGT):
            summed = jnp.zeros((rows_expert, D), jnp.float32)
            for quarter_id in range(N_LAYER):
                first = quarter_id * quarter
                partial_value = jnp.dot(latents[:, first:first + quarter], w_dec[target, expert, first:first + quarter], preferred_element_type=jnp.float32).astype(jnp.bfloat16)
                summed = summed + lax.optimization_barrier(partial_value).astype(jnp.float32)
            rebuilt.append(summed.astype(jnp.bfloat16))
        recon_sum = jnp.stack(rebuilt)
        recon_full = lax.optimization_barrier(recon_sum).astype(jnp.float32) + b_dec[:, None, :]
        recon_rows = recon_full.astype(jnp.bfloat16)
        wanted = targets_pad[:, expert_rows].astype(jnp.float32)
        live_rows = live_pad[expert_rows]
        error_grad = (coef * live_rows[None, :, None] * (recon_full - wanted)).astype(jnp.bfloat16)
        error_wide = lax.optimization_barrier(error_grad).astype(jnp.float32)
        bias_total = bias_total + lax.optimization_barrier(jnp.sum(error_wide, axis=1))
        latent_wide = latents.astype(jnp.float32)
        grad_dec = jnp.einsum('rl,trd->tld', latent_wide, error_wide)
        grad_latent = jnp.einsum('trd,tld->rl', error_wide, w_dec[:, expert].astype(jnp.float32))
        grad_pre = (grad_latent * (2.0 * active)).astype(jnp.bfloat16)
        grad_wide = lax.optimization_barrier(grad_pre).astype(jnp.float32)
        grad_enc = jnp.einsum('rd,rl->dl', inputs.astype(jnp.float32), grad_wide)
        grad_bias = lax.optimization_barrier(jnp.sum(grad_wide, axis=0))
        recon_out = recon_out.at[:, expert_rows].set(recon_rows)
        return ((recon_out, bias_total), (grad_enc.astype(jnp.bfloat16), grad_bias, grad_dec.astype(jnp.bfloat16)))
    initial = (jnp.zeros((TGT, TOKENS + 1, D), jnp.bfloat16), jnp.zeros((TGT, D), jnp.float32))
    (recon_out, bias_total), (grad_w_enc, grad_b_enc, grad_stack) = lax.scan(one_expert, initial, jnp.arange(EXPERTS, dtype=jnp.int32))
    grad_w_dec = jnp.swapaxes(grad_stack, 0, 1)
    return (recon_out[:, :TOKENS], grad_w_enc, grad_b_enc, grad_w_dec, bias_total)
```

```python
import math

import jax
import jax.numpy as jnp
from jax import lax
from jax.sharding import PartitionSpec as P

BF = jnp.bfloat16
F32 = jnp.float32
CHUNKS = 2


def dot(a, b):
    return jnp.dot(a, b, preferred_element_type=F32)


def local(tokens, expert_ids, slot_ids, live_mask, w_enc, b_enc, w_dec, b_dec, targets):
    n_expert = lax.axis_size("expert")
    n_layer = lax.axis_size("layer")
    n_dp = lax.axis_size("dp")
    layer = lax.axis_index("layer")
    core = lax.axis_index("dp")
    tok_rows, width = tokens.shape
    part = width // n_layer
    pair = 2 * part
    capacity = 2 * tok_rows // n_expert
    slots = capacity // CHUNKS
    rows = n_expert * slots
    lat = w_enc.shape[2]
    sign = 1 - 2 * core

    def ring(direction):
        pairs = []
        for l in range(n_layer):
            for d in range(n_dp):
                step = direction if d == 0 else -direction
                pairs.append((l * n_dp + d, (l + step) % n_layer * n_dp + d))
        return pairs

    along = lambda v: lax.ppermute(v, ("layer", "dp"), ring(1))
    against = lambda v: lax.ppermute(v, ("layer", "dp"), ring(-1))
    other_core = lambda v: lax.ppermute(v, "dp", [(0, 1), (1, 0)])

    order = [
        layer,
        (layer - sign + n_layer) % n_layer,
        (layer + sign + n_layer) % n_layer,
        (layer + 2) % n_layer,
    ]

    def gather(v):
        behind = along(v)
        ahead = against(v)
        opposite = along(behind)
        return [v, behind, ahead, opposite]

    def exchange(v):
        return lax.all_to_all(
            v.reshape(n_expert, slots, v.shape[-1]), "expert", split_axis=0, concat_axis=0, tiled=True
        ).reshape(rows, v.shape[-1])

    enc = w_enc[0]
    dec = w_dec[:, 0]
    enc_q = [lax.dynamic_slice(enc, (q * part, 0), (part, lat)) for q in order]
    dec_abs = jnp.stack(
        [
            jnp.concatenate([dec[0, :, q * part : (q + 1) * part], dec[1, :, q * part : (q + 1) * part]], axis=1)
            for q in range(n_layer)
        ]
    )
    dec_q = [lax.dynamic_index_in_dim(dec_abs, q, 0, keepdims=False) for q in order]
    targets_wide = jnp.concatenate([targets[0], targets[1]], axis=1)
    bias_wide = jnp.concatenate([b_dec[0], b_dec[1]])[None, :]

    own_quarter = lax.select_n(
        layer, *[tokens[:, q * part : (q + 1) * part] for q in range(n_layer)]
    )
    coef = 2.0 / math.sqrt(tok_rows)
    scale = coef * live_mask.astype(F32)[:, None]

    place = []
    for c in range(CHUNKS):
        low = slot_ids - c * slots
        cell = jnp.where((low >= 0) & (low < slots), expert_ids * slots + low, -1)
        place.append((lax.broadcasted_iota(jnp.int32, (rows, tok_rows), 0) == cell[None, :]).astype(BF))

    def error_of(recon_sum):
        full = recon_sum + bias_wide
        return full, (scale * (full - targets_wide.astype(F32))).astype(BF)

    xs, latents, actives, recon_sums, errs = [], [], [], [], []
    arrived = [exchange(dot(place[c], own_quarter).astype(BF)) for c in range(CHUNKS)]
    for c in range(CHUNKS):
        x = gather(arrived[c])
        xs.append(x)
        pre = dot(x[0], enc_q[0]) + dot(x[1], enc_q[1]) + dot(x[2], enc_q[2]) + dot(x[3], enc_q[3])
        active = jnp.maximum(pre + b_enc[0][None, :], 0.0)
        actives.append(active)
        latents.append((active * active).astype(BF))
    returned = []
    for c in range(CHUNKS):
        opposite = along(dot(latents[c], dec_q[3]).astype(BF))
        from_ahead = against(dot(latents[c], dec_q[1]).astype(BF))
        from_behind = along((dot(latents[c], dec_q[2]) + opposite.astype(F32)).astype(BF))
        total = dot(latents[c], dec_q[0]) + from_ahead.astype(F32) + from_behind.astype(F32)
        returned.append(exchange(total.astype(BF)))
    for c in range(CHUNKS):
        recon_sum = lax.dot_general(
            place[c], returned[c], (((0,), (0,)), ((), ())), preferred_element_type=F32
        )
        recon_sums.append(recon_sum)
        _, err = error_of(recon_sum)
        errs.append(gather(exchange(dot(place[c], err).astype(BF))))

    recon_full, err_all = error_of(sum(recon_sums[1:], recon_sums[0]))
    recon_wide = recon_full.astype(BF)
    recon = jnp.stack([recon_wide[:, :part], recon_wide[:, part:]])
    bias_sum = jnp.sum(lax.optimization_barrier(err_all).astype(F32), axis=0)
    bias_sum = jnp.stack([bias_sum[:part], bias_sum[part:]])
    bias_sum = bias_sum + other_core(bias_sum)
    bit = 1
    while bit < n_expert:
        bias_sum = bias_sum + lax.ppermute(bias_sum, "expert", [(i, i ^ bit) for i in range(n_expert)])
        bit *= 2

    def over_rows(a, b):
        return lax.dot_general(a, b, (((0,), (0,)), ((), ())), preferred_element_type=F32)

    grad_dec = jnp.stack(
        [sum(over_rows(latents[c], errs[c][k]) for c in range(CHUNKS)).astype(BF) for k in range(n_layer)]
    )
    grad_pres = []
    for c in range(CHUNKS):
        grad_latent = sum(
            lax.dot_general(errs[c][k], dec_q[k], (((1,), (1,)), ((), ())), preferred_element_type=F32)
            for k in range(n_layer)
        )
        grad_pres.append((grad_latent * (2.0 * actives[c])).astype(BF))
    grad_enc = jnp.stack(
        [sum(over_rows(xs[c][k], grad_pres[c]) for c in range(CHUNKS)).astype(BF) for k in range(n_layer)]
    )
    grad_bias = sum(jnp.sum(lax.optimization_barrier(g).astype(F32), axis=0) for g in grad_pres)

    half = n_layer // n_dp

    def position(q):
        ahead = (q - layer + n_layer) % n_layer
        return jnp.where(ahead == 0, 0, jnp.where(ahead == 2, 3, jnp.where(ahead == (sign + n_layer) % n_layer, 2, 1)))

    def share(stack):
        theirs = jnp.stack(
            [lax.dynamic_index_in_dim(stack, position((1 - core) * half + j), 0, keepdims=False) for j in range(half)]
        )
        mine = jnp.stack(
            [lax.dynamic_index_in_dim(stack, position(core * half + j), 0, keepdims=False) for j in range(half)]
        )
        return (mine.astype(F32) + other_core(theirs).astype(F32)).astype(BF)

    dec_share = share(grad_dec)
    enc_share = share(grad_enc)
    bias_parts = grad_bias.reshape(n_dp, lat // n_dp)
    bias_share = lax.dynamic_index_in_dim(bias_parts, core, 0) + other_core(
        lax.dynamic_index_in_dim(bias_parts, 1 - core, 0)
    )
    dec_out = jnp.stack(
        [
            jnp.concatenate([dec_share[j][:, t * part : (t + 1) * part] for j in range(half)], axis=1)
            for t in range(2)
        ]
    )
    return (
        recon,
        enc_share.reshape(1, half * part, lat),
        bias_share,
        dec_out[:, None],
        bias_sum,
    )


def solution(mesh):
    placed = (
        P(("expert", "dp"), None),
        P(("expert", "dp")),
        P(("expert", "dp")),
        P(("expert", "dp")),
        P("expert", None, "layer"),
        P("expert", "layer"),
        P(None, "expert", "layer", None),
        P(None, "layer"),
        P(None, ("expert", "dp"), "layer"),
    )
    return jax.shard_map(
        local,
        mesh=mesh,
        in_specs=placed,
        out_specs=(
            P(None, ("expert", "dp"), "layer"),
            P("expert", "dp", "layer"),
            P("expert", ("layer", "dp")),
            P(None, "expert", "layer", "dp"),
            P(None, "layer"),
        ),
        check_vma=False,
    )
```

```python
import math

import jax
import jax.numpy as jnp
from jax import lax
from jax.sharding import PartitionSpec as P

BF = jnp.bfloat16
F32 = jnp.float32
CHUNKS = 2


def dot(a, b):
    return jnp.dot(a, b, preferred_element_type=F32)


def local(tokens, expert_ids, slot_ids, live_mask, w_enc, b_enc, w_dec, b_dec, targets):
    n_expert = lax.axis_size("expert")
    n_layer = lax.axis_size("layer")
    n_dp = lax.axis_size("dp")
    layer = lax.axis_index("layer")
    core = lax.axis_index("dp")
    tok_rows, width = tokens.shape
    part = width // n_layer
    half = width // n_dp
    capacity = 2 * tok_rows // n_expert
    total = n_expert * capacity
    rows = total // CHUNKS
    lat = w_enc.shape[2]

    first_step = jnp.where(core == 0, 1, 3)
    second_step = jnp.where(core == 0, 3, 1)

    def neighbours(steps):
        return [
            (l * n_dp + d, (l ^ steps[d]) * n_dp + d) for l in range(n_layer) for d in range(n_dp)
        ]

    first = lambda v: lax.ppermute(v, ("layer", "dp"), neighbours((1, 3)))
    second = lambda v: lax.ppermute(v, ("layer", "dp"), neighbours((3, 1)))
    other_core = lambda v: lax.ppermute(v, "dp", [(0, 1), (1, 0)])
    order = [layer, layer ^ first_step, layer ^ second_step, layer ^ 2]

    def gather(v):
        a = first(v)
        b = second(v)
        return [v, a, b, second(a)]

    def exchange(v):
        return lax.all_to_all(
            v.reshape(n_expert, capacity, v.shape[-1]), "expert", split_axis=0, concat_axis=0, tiled=True
        ).reshape(n_expert * capacity, v.shape[-1])

    def after(v, done):
        return lax.optimization_barrier((v, done))[0]

    near = (layer // 2) == core
    low_side = layer < 2
    odd = (layer % 2) == 1

    def halves(v):
        own = jnp.where(near, v[0], v[3]), jnp.where(low_side, v[1], v[2])
        theirs = jnp.where(near, v[3], v[0]), jnp.where(low_side, v[2], v[1])
        ordered = lambda p: (jnp.where(odd, p[1], p[0]), jnp.where(odd, p[0], p[1]))
        return ordered(own), ordered(theirs)

    enc = w_enc[0]
    dec = w_dec[:, 0]
    coef = 2.0 / math.sqrt(tok_rows)

    cell = expert_ids * capacity + slot_ids
    place = (lax.broadcasted_iota(jnp.int32, (total, tok_rows), 0) == cell[None, :]).astype(BF)

    own_quarter = lax.select_n(
        layer, *[tokens[:, q * part : (q + 1) * part] for q in range(n_layer)]
    )
    flag = live_mask.astype(BF)[:, None]
    payload = jnp.concatenate([own_quarter, jnp.broadcast_to(flag, (tok_rows, 640 - part))], axis=1)
    targets_wide = jnp.concatenate([targets[0], targets[1]], axis=1)
    bias_wide = jnp.concatenate([b_dec[0], b_dec[1]])[None, :]

    arrived = exchange(dot(place, payload).astype(BF))
    wanted = exchange(after(dot(place, targets_wide).astype(BF), arrived))
    chunk = lambda v, c: v[c * rows : (c + 1) * rows]

    enc_q = [lax.dynamic_slice(enc, (q * part, 0), (part, lat)) for q in order]
    dec_abs = jnp.stack(
        [
            jnp.concatenate([dec[0, :, q * part : (q + 1) * part], dec[1, :, q * part : (q + 1) * part]], axis=1)
            for q in range(n_layer)
        ]
    )
    dec_q = [lax.dynamic_index_in_dim(dec_abs, q, 0, keepdims=False) for q in order]

    xs, latents, actives = [], [], []
    for c in range(CHUNKS):
        x = gather(chunk(arrived, c))
        xs.append(x)
        x = [v[:, :part] for v in x]
        pre = dot(x[0], enc_q[0]) + dot(x[1], enc_q[1]) + dot(x[2], enc_q[2]) + dot(x[3], enc_q[3])
        active = jnp.maximum(pre + b_enc[0][None, :], 0.0)
        actives.append(active)
        latents.append((active * active).astype(BF))

    recons, errs, bias_sums = [], [], []
    for c in range(CHUNKS):
        passed = first(dot(latents[c], dec_q[3]).astype(BF))
        from_first = first(dot(latents[c], dec_q[1]).astype(BF))
        from_second = second((dot(latents[c], dec_q[2]) + passed.astype(F32)).astype(BF))
        whole = dot(latents[c], dec_q[0]) + from_first.astype(F32) + from_second.astype(F32)
        recon_sum = lax.optimization_barrier(whole.astype(BF))
        recons.append(recon_sum)
        full = recon_sum.astype(F32) + bias_wide
        scale = coef * chunk(arrived, c)[:, part : part + 1].astype(F32)
        err = lax.optimization_barrier((scale * (full - chunk(wanted, c).astype(F32))).astype(BF))
        bias_sums.append(jnp.sum(err.astype(F32), axis=0))
        errs.append(gather(err))

    bias_sum = sum(bias_sums)
    bias_sum = (bias_sum + other_core(bias_sum)).reshape(2, part)
    bias_part = lax.dynamic_index_in_dim(bias_sum, core, 0, keepdims=False)
    coarse = lax.optimization_barrier(bias_part.astype(BF))
    fine = (bias_part - coarse.astype(F32)).astype(BF)
    extra = jnp.concatenate([coarse, fine, jnp.zeros((capacity * 128 - 2 * part,), BF)]).reshape(capacity, 128)
    extra = jnp.broadcast_to(extra[None], (n_expert, capacity, 128)).reshape(total, 128)
    returned = exchange(jnp.concatenate([jnp.concatenate(recons, axis=0), extra], axis=1))
    recon_sum = lax.dot_general(
        place, returned[:, : 2 * part], (((0,), (0,)), ((), ())), preferred_element_type=F32
    )
    recon_wide = (recon_sum + bias_wide).astype(BF)
    recon = jnp.stack([recon_wide[:, :part], recon_wide[:, part:]])
    extra = jnp.sum(returned[:, 2 * part :].reshape(n_expert, capacity, 128).astype(F32), axis=0).reshape(-1)
    bias_mine = extra[:part] + extra[part : 2 * part]
    bias_other = other_core(bias_mine)
    bias_sum = jnp.where(core == 0, jnp.stack([bias_mine, bias_other]), jnp.stack([bias_other, bias_mine]))

    x_own, x_theirs = [], []
    for c in range(CHUNKS):
        own, theirs = halves([v[:, :part] for v in after(xs[c], recons)])
        x_own.append(jnp.concatenate(own, axis=1))
        x_theirs.append(jnp.concatenate(theirs, axis=1))

    def over_rows(a, b):
        return lax.dot_general(a, b, (((0,), (0,)), ((), ())), preferred_element_type=F32)

    grad_dec = [0.0, 0.0]
    grad_enc = 0.0
    grad_bias = 0.0
    for c in range(CHUNKS):
        both_latents = jnp.concatenate([latents[c], other_core(latents[c])], axis=0)
        both_x = jnp.concatenate([x_own[c], other_core(x_theirs[c])], axis=0)
        own, theirs = halves(errs[c])
        arrange = lambda p, t: jnp.concatenate([v[:, t * part : (t + 1) * part] for v in p], axis=1)
        sent = other_core(jnp.stack([arrange(theirs, t) for t in range(2)]))
        for t in range(2):
            both = jnp.concatenate([arrange(own, t), sent[t]], axis=0)
            grad_dec[t] = grad_dec[t] + over_rows(both_latents, both)
        grad_latent = sum(
            lax.dot_general(errs[c][k], dec_q[k], (((1,), (1,)), ((), ())), preferred_element_type=F32)
            for k in range(n_layer)
        )
        grad_pre = (grad_latent * (2.0 * actives[c])).astype(BF)
        both_pre = jnp.concatenate([grad_pre, other_core(grad_pre)], axis=0)
        grad_enc = grad_enc + over_rows(both_x, both_pre)
        grad_bias = grad_bias + jnp.sum(lax.optimization_barrier(both_pre).astype(F32), axis=0)

    bias_share = lax.dynamic_index_in_dim(grad_bias.reshape(n_dp, lat // n_dp), core, 0)
    return (
        recon,
        grad_enc.astype(BF)[None],
        bias_share,
        jnp.stack(grad_dec).astype(BF)[:, None],
        bias_sum,
    )


def solution(mesh):
    placed = (
        P(("expert", "dp"), None),
        P(("expert", "dp")),
        P(("expert", "dp")),
        P(("expert", "dp")),
        P("expert", None, "layer"),
        P("expert", "layer"),
        P(None, "expert", "layer", None),
        P(None, "layer"),
        P(None, ("expert", "dp"), "layer"),
    )
    return jax.shard_map(
        local,
        mesh=mesh,
        in_specs=placed,
        out_specs=(
            P(None, ("expert", "dp"), "layer"),
            P("expert", "dp", "layer"),
            P("expert", ("layer", "dp")),
            P(None, "expert", "layer", "dp"),
            P(None, "layer"),
        ),
        check_vma=False,
    )
```

```python
import math

import jax
import jax.numpy as jnp
from jax import lax
from jax.experimental import pallas as pl
from jax.experimental.pallas import tpu as pltpu
from jax.sharding import PartitionSpec as P

BF = jnp.bfloat16
F32 = jnp.float32
CHUNKS = 2


def dot(a, b):
    return jnp.dot(a, b, preferred_element_type=F32)


def arrange_kernel(where_ref, v_ref, a_ref, b_ref, c_ref, own_ref, theirs_ref):
    near, low_side, odd = where_ref[0] == 1, where_ref[1] == 1, where_ref[2] == 1
    targets_count, _, half = own_ref.shape
    part = half // 2
    for t in range(targets_count):
        cols = slice(t * part, (t + 1) * part)
        v, a, b, c = (r[:, cols] for r in (v_ref, a_ref, b_ref, c_ref))
        for out, pair in (
            (own_ref, (jnp.where(near, v, c), jnp.where(low_side, a, b))),
            (theirs_ref, (jnp.where(near, c, v), jnp.where(low_side, b, a))),
        ):
            out[t, :, :part] = jnp.where(odd, pair[1], pair[0])
            out[t, :, part:] = jnp.where(odd, pair[0], pair[1])


def arrange(where, blocks, targets_count, part):
    rows, width = blocks[0].shape
    tile = rows // 4
    out = jax.ShapeDtypeStruct((targets_count, rows, 2 * part), BF)
    return pl.pallas_call(
        arrange_kernel,
        name="arrange",
        cost_estimate=pl.CostEstimate(flops=0, bytes_accessed=16 * rows * targets_count * part, transcendentals=0),
        compiler_params=pltpu.CompilerParams(vmem_limit_bytes=8 * 2**20),
        out_shape=(out, out),
        grid_spec=pltpu.PrefetchScalarGridSpec(
            num_scalar_prefetch=1,
            grid=(4,),
            in_specs=[pl.BlockSpec((tile, width), lambda i, w: (i, 0))] * 4,
            out_specs=[pl.BlockSpec((targets_count, tile, 2 * part), lambda i, w: (0, i, 0))] * 2,
        ),
    )(where, *blocks)


def local(tokens, expert_ids, slot_ids, live_mask, w_enc, b_enc, w_dec, b_dec, targets):
    n_expert = lax.axis_size("expert")
    n_layer = lax.axis_size("layer")
    n_dp = lax.axis_size("dp")
    layer = lax.axis_index("layer")
    core = lax.axis_index("dp")
    tok_rows, width = tokens.shape
    part = width // n_layer
    half = width // n_dp
    capacity = 2 * tok_rows // n_expert
    total = n_expert * capacity
    rows = total // CHUNKS
    lat = w_enc.shape[2]

    first_step = jnp.where(core == 0, 1, 3)
    second_step = jnp.where(core == 0, 3, 1)

    def neighbours(steps):
        return [
            (l * n_dp + d, (l ^ steps[d]) * n_dp + d) for l in range(n_layer) for d in range(n_dp)
        ]

    first = lambda v: lax.ppermute(v, ("layer", "dp"), neighbours((1, 3)))
    second = lambda v: lax.ppermute(v, ("layer", "dp"), neighbours((3, 1)))
    other_core = lambda v: lax.ppermute(v, "dp", [(0, 1), (1, 0)])
    order = [layer, layer ^ first_step, layer ^ second_step, layer ^ 2]

    def gather(v):
        a = first(v)
        b = second(v)
        return [v, a, b, second(a)]

    def exchange(v):
        return lax.all_to_all(
            v.reshape(n_expert, capacity, v.shape[-1]), "expert", split_axis=0, concat_axis=0, tiled=True
        ).reshape(n_expert * capacity, v.shape[-1])

    def after(v, done):
        return lax.optimization_barrier((v, done))[0]

    where = jnp.stack([(layer // 2) == core, layer < 2, (layer % 2) == 1]).astype(jnp.int32)

    enc = w_enc[0]
    dec = w_dec[:, 0]
    coef = 2.0 / math.sqrt(tok_rows)

    cell = expert_ids * capacity + slot_ids
    place = (lax.broadcasted_iota(jnp.int32, (total, tok_rows), 0) == cell[None, :]).astype(BF)

    own_quarter = lax.select_n(
        layer, *[tokens[:, q * part : (q + 1) * part] for q in range(n_layer)]
    )
    flag = live_mask.astype(BF)[:, None]
    payload = jnp.concatenate([own_quarter, jnp.broadcast_to(flag, (tok_rows, 640 - part))], axis=1)
    targets_wide = jnp.concatenate([targets[0], targets[1]], axis=1)
    bias_wide = jnp.concatenate([b_dec[0], b_dec[1]])[None, :]

    arrived = exchange(dot(place, payload).astype(BF))
    chunk = lambda v, c: v[c * rows : (c + 1) * rows]
    xs = [gather(chunk(arrived, c)) for c in range(CHUNKS)]
    wanted = exchange(after(dot(place, targets_wide).astype(BF), xs[0][1]))

    enc_q = [lax.dynamic_slice(enc, (q * part, 0), (part, lat)) for q in order]
    dec_abs = jnp.stack(
        [
            jnp.concatenate([dec[0, :, q * part : (q + 1) * part], dec[1, :, q * part : (q + 1) * part]], axis=1)
            for q in range(n_layer)
        ]
    )
    dec_q = [lax.dynamic_index_in_dim(dec_abs, q, 0, keepdims=False) for q in order]

    latents, actives = [], []
    for c in range(CHUNKS):
        x = [v[:, :part] for v in xs[c]]
        pre = dot(x[0], enc_q[0]) + dot(x[1], enc_q[1]) + dot(x[2], enc_q[2]) + dot(x[3], enc_q[3])
        active = jnp.maximum(pre + b_enc[0][None, :], 0.0)
        actives.append(active)
        latents.append((active * active).astype(BF))

    x_own, x_theirs = [], []
    for c in range(CHUNKS):
        own, theirs = arrange(where, after(xs[c], latents), 1, part)
        x_own.append(own[0])
        x_theirs.append(theirs[0])

    recons, errs, bias_sums = [], [], []
    for c in range(CHUNKS):
        passed = first(dot(latents[c], dec_q[3]).astype(BF))
        from_first = first(dot(latents[c], dec_q[1]).astype(BF))
        from_second = second((dot(latents[c], dec_q[2]) + passed.astype(F32)).astype(BF))
        whole = dot(after(latents[c], x_own), dec_q[0]) + from_first.astype(F32) + from_second.astype(F32)
        recon_sum = lax.optimization_barrier(whole.astype(BF))
        recons.append(recon_sum)
        full = recon_sum.astype(F32) + bias_wide
        scale = coef * chunk(arrived, c)[:, part : part + 1].astype(F32)
        err = lax.optimization_barrier((scale * (full - chunk(wanted, c).astype(F32))).astype(BF))
        bias_sums.append(jnp.sum(err.astype(F32), axis=0))
        errs.append(gather(err))

    bias_sum = sum(bias_sums)
    bias_sum = (bias_sum + other_core(bias_sum)).reshape(2, part)
    bias_part = lax.dynamic_index_in_dim(bias_sum, core, 0, keepdims=False)
    coarse = lax.optimization_barrier(bias_part.astype(BF))
    fine = (bias_part - coarse.astype(F32)).astype(BF)
    extra = jnp.concatenate([coarse, fine, jnp.zeros((capacity * 128 - 2 * part,), BF)]).reshape(capacity, 128)
    extra = jnp.broadcast_to(extra[None], (n_expert, capacity, 128)).reshape(total, 128)
    returned = exchange(jnp.concatenate([jnp.concatenate(recons, axis=0), extra], axis=1))
    recon_sum = lax.dot_general(
        place, returned, (((0,), (0,)), ((), ())), preferred_element_type=F32
    )[:, : 2 * part]
    recon_wide = (recon_sum + bias_wide).astype(BF)
    recon = jnp.stack([recon_wide[:, :part], recon_wide[:, part:]])
    extra = jnp.sum(returned[:, 2 * part :].reshape(n_expert, capacity, 128).astype(F32), axis=0).reshape(-1)
    bias_mine = extra[:part] + extra[part : 2 * part]
    bias_other = other_core(bias_mine)
    bias_sum = jnp.where(core == 0, jnp.stack([bias_mine, bias_other]), jnp.stack([bias_other, bias_mine]))

    def over_rows(a, b):
        return lax.dot_general(a, b, (((0,), (0,)), ((), ())), preferred_element_type=F32)

    err_own, err_theirs, pre_own, pre_theirs = [], [], [], []
    for c in range(CHUNKS):
        own, theirs = arrange(where, errs[c], 2, part)
        err_own.append(own)
        err_theirs.append(other_core(theirs))
        grad_latent = sum(
            lax.dot_general(errs[c][k], dec_q[k], (((1,), (1,)), ((), ())), preferred_element_type=F32)
            for k in range(n_layer)
        )
        grad_pre = (grad_latent * (2.0 * actives[c])).astype(BF)
        pre_own.append(grad_pre)
        pre_theirs.append(other_core(grad_pre))
    join = lambda own, theirs: jnp.concatenate(own + theirs, axis=0)
    all_x = join(x_own, [other_core(v) for v in x_theirs])
    all_latents = join(latents, [other_core(v) for v in latents])
    all_pre = lax.optimization_barrier(join(pre_own, pre_theirs))
    grad_enc = over_rows(all_x, all_pre)
    grad_bias = jnp.sum(all_pre.astype(F32), axis=0)
    grad_dec = [over_rows(all_latents, join([v[t] for v in err_own], [v[t] for v in err_theirs])) for t in range(2)]

    bias_share = lax.dynamic_index_in_dim(grad_bias.reshape(n_dp, lat // n_dp), core, 0)
    return (
        recon,
        grad_enc.astype(BF)[None],
        bias_share,
        jnp.stack(grad_dec).astype(BF)[:, None],
        bias_sum,
    )


def solution(mesh):
    placed = (
        P(("expert", "dp"), None),
        P(("expert", "dp")),
        P(("expert", "dp")),
        P(("expert", "dp")),
        P("expert", None, "layer"),
        P("expert", "layer"),
        P(None, "expert", "layer", None),
        P(None, "layer"),
        P(None, ("expert", "dp"), "layer"),
    )
    return jax.shard_map(
        local,
        mesh=mesh,
        in_specs=placed,
        out_specs=(
            P(None, ("expert", "dp"), "layer"),
            P("expert", "dp", "layer"),
            P("expert", ("layer", "dp")),
            P(None, "expert", "layer", "dp"),
            P(None, "layer"),
        ),
        check_vma=False,
    )
```

```python
import math

import jax
import jax.numpy as jnp
from jax import lax
from jax.experimental import pallas as pl
from jax.experimental.pallas import tpu as pltpu
from jax.sharding import PartitionSpec as P

BF = jnp.bfloat16
F32 = jnp.float32
CHUNKS = 2


def dot(a, b):
    return jnp.dot(a, b, preferred_element_type=F32)


def arrange_kernel(where_ref, v_ref, a_ref, b_ref, c_ref, *outs):
    near, low_side, odd = where_ref[0] == 1, where_ref[1] == 1, where_ref[2] == 1
    targets_count = len(outs) // 2
    part = outs[0].shape[1] // 2
    for t in range(targets_count):
        cols = slice(t * part, (t + 1) * part)
        v, a, b, c = (r[:, cols] for r in (v_ref, a_ref, b_ref, c_ref))
        for out, pair in (
            (outs[t], (jnp.where(near, v, c), jnp.where(low_side, a, b))),
            (outs[targets_count + t], (jnp.where(near, c, v), jnp.where(low_side, b, a))),
        ):
            out[:, :part] = jnp.where(odd, pair[1], pair[0])
            out[:, part:] = jnp.where(odd, pair[0], pair[1])


def arrange(where, blocks, targets_count, part):
    rows, width = blocks[0].shape
    tile = rows // 4
    count = 2 * targets_count
    out = pl.pallas_call(
        arrange_kernel,
        name="arrange",
        cost_estimate=pl.CostEstimate(flops=0, bytes_accessed=16 * rows * targets_count * part, transcendentals=0),
        compiler_params=pltpu.CompilerParams(vmem_limit_bytes=8 * 2**20),
        out_shape=[jax.ShapeDtypeStruct((rows, 2 * part), BF)] * count,
        grid_spec=pltpu.PrefetchScalarGridSpec(
            num_scalar_prefetch=1,
            grid=(4,),
            in_specs=[pl.BlockSpec((tile, width), lambda i, w: (i, 0))] * 4,
            out_specs=[pl.BlockSpec((tile, 2 * part), lambda i, w: (i, 0))] * count,
        ),
    )(where, *blocks)
    return out[:targets_count], out[targets_count:]


def local(tokens, expert_ids, slot_ids, live_mask, w_enc, b_enc, w_dec, b_dec, targets):
    n_expert = lax.axis_size("expert")
    n_layer = lax.axis_size("layer")
    n_dp = lax.axis_size("dp")
    layer = lax.axis_index("layer")
    core = lax.axis_index("dp")
    tok_rows, width = tokens.shape
    part = width // n_layer
    half = width // n_dp
    capacity = 2 * tok_rows // n_expert
    total = n_expert * capacity
    rows = total // CHUNKS
    lat = w_enc.shape[2]

    first_step = jnp.where(core == 0, 1, 3)
    second_step = jnp.where(core == 0, 3, 1)

    def neighbours(steps):
        return [
            (l * n_dp + d, (l ^ steps[d]) * n_dp + d) for l in range(n_layer) for d in range(n_dp)
        ]

    first = lambda v: lax.ppermute(v, ("layer", "dp"), neighbours((1, 3)))
    second = lambda v: lax.ppermute(v, ("layer", "dp"), neighbours((3, 1)))
    other_core = lambda v: lax.ppermute(v, "dp", [(0, 1), (1, 0)])
    order = [layer, layer ^ first_step, layer ^ second_step, layer ^ 2]

    def gather(v):
        a = first(v)
        b = second(v)
        return [v, a, b, second(a)]

    def exchange(v):
        return lax.all_to_all(
            v.reshape(n_expert, capacity, v.shape[-1]), "expert", split_axis=0, concat_axis=0, tiled=True
        ).reshape(n_expert * capacity, v.shape[-1])

    def after(v, done):
        return lax.optimization_barrier((v, done))[0]

    where = jnp.stack([(layer // 2) == core, layer < 2, (layer % 2) == 1]).astype(jnp.int32)

    enc = w_enc[0]
    dec = w_dec[:, 0]
    coef = 2.0 / math.sqrt(tok_rows)

    cell = expert_ids * capacity + slot_ids
    place = (lax.broadcasted_iota(jnp.int32, (total, tok_rows), 0) == cell[None, :]).astype(BF)

    own_quarter = lax.select_n(
        layer, *[tokens[:, q * part : (q + 1) * part] for q in range(n_layer)]
    )
    flag = live_mask.astype(BF)[:, None]
    payload = jnp.concatenate([own_quarter, jnp.broadcast_to(flag, (tok_rows, 640 - part))], axis=1)
    targets_wide = jnp.concatenate([targets[0], targets[1]], axis=1)
    bias_wide = jnp.concatenate([b_dec[0], b_dec[1]])[None, :]

    arrived = exchange(dot(place, payload).astype(BF))
    chunk = lambda v, c: v[c * rows : (c + 1) * rows]
    xs = [gather(chunk(arrived, c)) for c in range(CHUNKS)]
    wanted = exchange(after(dot(place, targets_wide).astype(BF), xs[0][1]))

    enc_q = [lax.dynamic_slice(enc, (q * part, 0), (part, lat)) for q in order]
    dec_abs = jnp.stack(
        [
            jnp.concatenate([dec[0, :, q * part : (q + 1) * part], dec[1, :, q * part : (q + 1) * part]], axis=1)
            for q in range(n_layer)
        ]
    )
    dec_q = [lax.dynamic_index_in_dim(dec_abs, q, 0, keepdims=False) for q in order]

    latents, actives = [], []
    for c in range(CHUNKS):
        x = [v[:, :part] for v in xs[c]]
        pre = dot(x[0], enc_q[0]) + dot(x[1], enc_q[1]) + dot(x[2], enc_q[2]) + dot(x[3], enc_q[3])
        active = jnp.maximum(pre + b_enc[0][None, :], 0.0)
        actives.append(active)
        latents.append((active * active).astype(BF))

    x_own, x_theirs = [], []
    for c in range(CHUNKS):
        own, theirs = arrange(where, after(xs[c], latents), 1, part)
        x_own.append(own[0])
        x_theirs.append(theirs[0])

    recons, errs, bias_sums = [], [], []
    for c in range(CHUNKS):
        passed = first(dot(latents[c], dec_q[3]).astype(BF))
        from_first = first(dot(latents[c], dec_q[1]).astype(BF))
        from_second = second((dot(latents[c], dec_q[2]) + passed.astype(F32)).astype(BF))
        whole = dot(after(latents[c], x_own), dec_q[0]) + from_first.astype(F32) + from_second.astype(F32)
        recon_sum = lax.optimization_barrier(whole.astype(BF))
        recons.append(recon_sum)
        full = recon_sum.astype(F32) + bias_wide
        scale = coef * chunk(arrived, c)[:, part : part + 1].astype(F32)
        err = lax.optimization_barrier((scale * (full - chunk(wanted, c).astype(F32))).astype(BF))
        bias_sums.append(jnp.sum(err.astype(F32), axis=0))
        errs.append(gather(err))

    bias_sum = sum(bias_sums)
    bias_sum = (bias_sum + other_core(bias_sum)).reshape(2, part)
    bias_part = lax.dynamic_index_in_dim(bias_sum, core, 0, keepdims=False)
    coarse = lax.optimization_barrier(bias_part.astype(BF))
    fine = (bias_part - coarse.astype(F32)).astype(BF)
    extra = jnp.concatenate([coarse, fine, jnp.zeros((capacity * 128 - 2 * part,), BF)]).reshape(capacity, 128)
    extra = jnp.broadcast_to(extra[None], (n_expert, capacity, 128)).reshape(total, 128)
    returned = exchange(jnp.concatenate([jnp.concatenate(recons, axis=0), extra], axis=1))
    recon_sum = lax.dot_general(
        place, returned, (((0,), (0,)), ((), ())), preferred_element_type=F32
    )[:, : 2 * part]
    recon_wide = (recon_sum + bias_wide).astype(BF)
    recon = jnp.stack([recon_wide[:, :part], recon_wide[:, part:]])
    extra = jnp.sum(returned[:, 2 * part :].reshape(n_expert, capacity, 128).astype(F32), axis=0).reshape(-1)
    bias_mine = extra[:part] + extra[part : 2 * part]
    bias_other = other_core(bias_mine)
    bias_sum = jnp.where(core == 0, jnp.stack([bias_mine, bias_other]), jnp.stack([bias_other, bias_mine]))

    def over_rows(a, b):
        return lax.dot_general(a, b, (((0,), (0,)), ((), ())), preferred_element_type=F32)

    err_own, err_theirs, pre_own, pre_theirs = [], [], [], []
    for c in range(CHUNKS):
        own, theirs = arrange(where, errs[c], 2, part)
        err_own.append(own)
        err_theirs.append([other_core(v) for v in theirs])
        grad_latent = sum(
            lax.dot_general(errs[c][k], dec_q[k], (((1,), (1,)), ((), ())), preferred_element_type=F32)
            for k in range(n_layer)
        )
        grad_pre = (grad_latent * (2.0 * actives[c])).astype(BF)
        pre_own.append(grad_pre)
        pre_theirs.append(other_core(grad_pre))
    join = lambda own, theirs: jnp.concatenate(own + theirs, axis=0)
    all_x = join(x_own, [other_core(v) for v in x_theirs])
    all_latents = join(latents, [other_core(v) for v in latents])
    all_pre = lax.optimization_barrier(join(pre_own, pre_theirs))
    grad_enc = over_rows(all_x, all_pre)
    grad_bias = jnp.sum(all_pre.astype(F32), axis=0)
    grad_dec = [over_rows(all_latents, join([v[t] for v in err_own], [v[t] for v in err_theirs])) for t in range(2)]

    bias_share = lax.dynamic_index_in_dim(grad_bias.reshape(n_dp, lat // n_dp), core, 0)
    return (
        recon,
        grad_enc.astype(BF)[None],
        bias_share,
        jnp.stack(grad_dec).astype(BF)[:, None],
        bias_sum,
    )


def solution(mesh):
    placed = (
        P(("expert", "dp"), None),
        P(("expert", "dp")),
        P(("expert", "dp")),
        P(("expert", "dp")),
        P("expert", None, "layer"),
        P("expert", "layer"),
        P(None, "expert", "layer", None),
        P(None, "layer"),
        P(None, ("expert", "dp"), "layer"),
    )
    return jax.shard_map(
        local,
        mesh=mesh,
        in_specs=placed,
        out_specs=(
            P(None, ("expert", "dp"), "layer"),
            P("expert", "dp", "layer"),
            P("expert", ("layer", "dp")),
            P(None, "expert", "layer", "dp"),
            P(None, "layer"),
        ),
        check_vma=False,
    )
```
